32 devices in a mesh: across: 4 (over y, x), along: 8 (over z, core).
Axes of the slice: x: 2, y: 2, z: 4, core: 2. Of those that a mesh axis runs over, the one named last changes fastest.
Arguments:
- radiance: bfloat16 [224, 128, 2048], P(None, 'along', 'across'), as said below
- kernel_one: float32 [224, 25], replicated, may hold values from 0 to 0.08
- kernel_two: float32 [224, 25], replicated, may hold values from 0 to 0.08
- usable_mask: int32 [128, 2048], P('along', 'across'), may hold values from 0 to 1, as said below
Outputs:
- anomaly_score: float32 [128, 2048], P('along', 'across')
The draws below stay inside these ranges and needn't reach their ends.
Inputs may be any that keep to these rules, and one draw needn't show every extreme that they name: `usable_mask`: 1 marks a pixel that enters the statistics and is scored, 0 one that is left out. Calibrated radiance, finite.
All inputs are finite; a program needn't handle non-finite values.
Results may differ from the reference program's by a relative error of at most 0.0019.
Values may be sent and summed in bfloat16 or wider, within the bound.
A program may use at most 128 MiB of HBM per device.

```python
import math
import jax
import jax.numpy as jnp
from jax import lax

BANDS = 224
KSIZE = 5
TILE_ROWS = 16
NROWS = 128
NCOLS = 2048
N_ALONG = 8


def draw_radiance(key, part):
    keys = jax.random.split(key, 4)
    base_noise = jax.random.normal(keys[0], (BANDS + 1, NROWS, NCOLS), jnp.float32)
    common_weight = 0.5
    common = jax.random.normal(keys[1], (1, NROWS, NCOLS), jnp.float32)
    band_scale = jnp.exp(jax.random.uniform(keys[2], (BANDS, 1, 1), jnp.float32, 0.0, math.log(10.0)))
    band_offset = jax.random.uniform(keys[3], (BANDS, 1, 1), jnp.float32, -1.0, 1.0)
    ramp = 1.0 + 2.0 * jnp.arange(NROWS, dtype=jnp.float32) / max(NROWS - 1, 1)
    spectra = base_noise[1:] + 0.6 * base_noise[:-1] + common_weight * common
    values = band_offset + band_scale * ramp[None, :, None] * spectra
    return values.astype(jnp.bfloat16)


def draw_usable_mask(key, part):
    ticket = jax.random.randint(key, (NROWS, NCOLS), 0, 1000)
    row_index = jnp.arange(NROWS, dtype=jnp.int32)[:, None]
    limit = 300 + 600 * row_index // max(NROWS - 1, 1)
    return (ticket < limit).astype(jnp.int32)


def setup_inputs(seed: int = 0) -> dict:
    key_list = jax.random.split(jax.random.key(seed), 5)
    radiance = draw_radiance(jax.random.fold_in(key_list[4], 71), 0)
    kernel_one = jnp.clip(jax.random.uniform(key_list[1], (BANDS, KSIZE * KSIZE), jnp.float32, 0.0, 0.08), 0.0, 0.08)
    kernel_two = jnp.clip(jax.random.uniform(key_list[2], (BANDS, KSIZE * KSIZE), jnp.float32, 0.0, 0.08), 0.0, 0.08)
    usable_mask = draw_usable_mask(jax.random.fold_in(key_list[4], 71), 0)
    return {"radiance": radiance, "kernel_one": kernel_one, "kernel_two": kernel_two, "usable_mask": usable_mask}


def smooth(padded, kernel, out_rows, out_cols):
    total = jnp.zeros((padded.shape[0], out_rows, out_cols), jnp.float32)
    for tap in range(KSIZE * KSIZE):
        row_off, col_off = divmod(tap, KSIZE)
        window = padded[:, row_off:row_off + out_rows, col_off:col_off + out_cols]
        total = total + kernel[:, tap][:, None, None] * window
    return total

def reference(radiance, kernel_one, kernel_two, usable_mask):
    band_count = radiance.shape[0]
    reach = KSIZE // 2
    widths = ((0, 0), (reach, reach), (reach, reach))

    def one_group(pieces):
        plane, first_taps, second_taps = pieces
        section_one = smooth(jnp.pad(plane.astype(jnp.float32), widths), first_taps, NROWS, NCOLS)
        section_two = smooth(jnp.pad(section_one, widths), second_taps, NROWS, NCOLS)
        return section_two.astype(jnp.bfloat16)
    groups = lax.map(one_group, (radiance.reshape(band_count // 8, 8, NROWS, NCOLS), kernel_one.reshape(band_count // 8, 8, KSIZE * KSIZE), kernel_two.reshape(band_count // 8, 8, KSIZE * KSIZE)))
    smoothed = groups.reshape(band_count, NROWS, NCOLS)
    masked = smoothed * usable_mask.astype(jnp.bfloat16)[None]
    flat = masked.reshape(band_count, NROWS * NCOLS)
    count = jnp.sum(usable_mask.astype(jnp.float32))
    band_sum = lax.optimization_barrier(jnp.sum(flat, axis=1, dtype=jnp.float32))
    gram = jnp.dot(flat.astype(jnp.float32), flat.T.astype(jnp.float32), preferred_element_type=jnp.float32)
    global_mean = band_sum / count
    covariance = (gram - count * jnp.outer(global_mean, global_mean)) / (count - 1.0)
    loading = 0.01 * jnp.trace(covariance) / band_count
    loaded = covariance + loading * jnp.eye(band_count, dtype=jnp.float32)
    lower = jnp.linalg.cholesky(loaded)
    whitener = lax.linalg.triangular_solve(lower, jnp.eye(band_count, dtype=jnp.float32), left_side=True, lower=True)

    def score_block(index):
        start = (index * TILE_ROWS).astype(jnp.int32)
        block = lax.dynamic_slice_in_dim(smoothed, start, TILE_ROWS, axis=1)
        centered = block.astype(jnp.float32).reshape(band_count, TILE_ROWS * NCOLS) - global_mean[:, None]
        whitened = jnp.dot(whitener.astype(jnp.float32), centered.astype(jnp.float32), precision=lax.Precision.HIGHEST, preferred_element_type=jnp.float32)
        return lax.optimization_barrier(jnp.sum(whitened * whitened, axis=0)).reshape(TILE_ROWS, NCOLS)
    blocks = lax.map(score_block, jnp.arange(N_ALONG, dtype=jnp.int32))
    distance = blocks.reshape(NROWS, NCOLS)
    standard = (distance - band_count) / math.sqrt(2.0 * band_count)
    return standard * usable_mask.astype(jnp.float32)
```

```python
import functools
import math

import jax
import jax.numpy as jnp
import numpy as np
from jax import lax
from jax.experimental import pallas as pl
from jax.experimental.pallas import tpu as pltpu
from jax.sharding import PartitionSpec as P

KSIZE = 5
REACH = KSIZE // 2
HALO = 2 * REACH
GROUP = 16
SIDE = 256
MESH_ID = pl.DeviceIdType.MESH


def row_orders(rows):
    packed_in = list(range(rows)) + list(range(-HALO, 0)) + list(range(rows, rows + HALO))
    packed_mid = list(range(rows)) + list(range(-REACH, 0)) + list(range(rows, rows + REACH))
    packed_mid += [None] * (-len(packed_mid) % 8)
    return packed_in, packed_mid


def tap_selector(out_order, in_order):
    select = np.zeros((KSIZE, KSIZE * len(out_order), len(in_order)), np.float32)
    for q in range(KSIZE):
        for m, r in enumerate(out_order):
            for k, s in enumerate(in_order):
                if r is not None and s is not None and 0 <= s - r + REACH < KSIZE:
                    select[s - r + REACH, q * len(out_order) + m, k] = 1.0
    return select


def tap_matrix(kernel, out_order, in_order, parts, width):
    bands = kernel.shape[0]
    high = lax.reduce_precision(kernel, 8, 7)
    low = kernel - high
    one = tap_selector(out_order, in_order)
    select = np.zeros((KSIZE, one.shape[1], width), np.float32)
    is_low = np.zeros((1, 1, width), bool)
    n = len(in_order)
    for i, part in enumerate(parts):
        select[:, :, i * n : (i + 1) * n] = one
        is_low[:, :, i * n : (i + 1) * n] = part == "low"

    def spread(taps, p):
        row = taps[:, p * KSIZE : (p + 1) * KSIZE]
        return jnp.repeat(row, len(out_order), axis=1)[:, :, None]

    total = jnp.zeros((bands, one.shape[1], width), jnp.float32)
    for p in range(KSIZE):
        total = total + select[p][None] * jnp.where(is_low, spread(low, p), spread(high, p))
    return total.astype(jnp.bfloat16)


def smooth_kernel(main_ref, halo_ref, edge_ref, first_ref, second_ref, keep_ref, out_ref, hold):
    rows, cols = main_ref.shape[1:]
    wide = cols + edge_ref.shape[2]
    mid = keep_ref.shape[0]

    def gather_columns(product, count):
        total = product[REACH * count : (REACH + 1) * count, :]
        for q in range(KSIZE):
            if q != REACH:
                total = total + pltpu.roll(
                    product[q * count : (q + 1) * count, :], (REACH - q) % wide, 1
                )
        return total

    def one_band(b, carry):
        main = jnp.concatenate([main_ref[b], edge_ref[b]], axis=1).astype(jnp.float32)
        packed = jnp.concatenate([main, halo_ref[b].astype(jnp.float32)], axis=0)
        packed = jnp.concatenate([packed, packed], axis=0).astype(jnp.bfloat16)
        product = jnp.dot(first_ref[b], packed, preferred_element_type=jnp.float32)
        section = gather_columns(product, mid) * keep_ref[...]
        high = section.astype(jnp.bfloat16).astype(jnp.float32)
        low = section - high
        spare = second_ref.shape[2] - 3 * mid
        packed = jnp.concatenate(
            [high, low, high, jnp.zeros((spare, wide), jnp.float32)], axis=0
        ).astype(jnp.bfloat16)
        product = jnp.dot(second_ref[b], packed, preferred_element_type=jnp.float32)
        result = gather_columns(product, rows)
        for j in range(cols // 128):
            hold[j, pl.ds(pl.multiple_of(b * rows, rows), rows), :] = result[:, j * 128 : j * 128 + 128]
        return carry

    lax.fori_loop(0, GROUP, one_band, 0, unroll=4)
    for r in range(rows):
        for j in range(cols // 128):
            out_ref[r, :, j * 128 : j * 128 + 128] = hold[
                j, pl.ds(r, GROUP, stride=rows), :
            ].astype(jnp.bfloat16)


def smooth_twice(radiance, halo, edge, first, second, keep):
    bands, rows, cols = radiance.shape

    def band_block(array):
        return pl.BlockSpec((GROUP,) + array.shape[1:], lambda i: (i, 0, 0))

    return pl.pallas_call(
        smooth_kernel,
        grid=(bands // GROUP,),
        out_shape=jax.ShapeDtypeStruct((rows, bands, cols), jnp.bfloat16),
        in_specs=[band_block(a) for a in (radiance, halo, edge, first, second)]
        + [pl.BlockSpec(keep.shape, lambda i: (0, 0))],
        out_specs=pl.BlockSpec((rows, GROUP, cols), lambda i: (0, i, 0)),
        scratch_shapes=[pltpu.VMEM((cols // 128, GROUP * rows, 128), jnp.float32)],
        compiler_params=pltpu.CompilerParams(vmem_limit_bytes=40 << 20),
        name="smooth_twice",
    )(radiance, halo, edge, first, second, keep)


def gram_kernel(x_ref, mask_ref, out_ref):
    step = pl.program_id(0)
    bands, cols = x_ref.shape[1:]
    per = x_ref.shape[0]

    @pl.when(step == 0)
    def _():
        out_ref[...] = jnp.zeros_like(out_ref)

    first = lax.broadcasted_iota(jnp.int32, (SIDE - bands, cols), 0) == 0
    total = jnp.zeros((SIDE, SIDE), jnp.float32)
    for r in range(per):
        line = mask_ref[r : r + 1, :].astype(jnp.float32)
        used = jnp.broadcast_to(line, (bands, cols)).astype(jnp.bfloat16)
        ones = jnp.where(first, jnp.broadcast_to(line, first.shape), 0.0).astype(jnp.bfloat16)
        block = jnp.concatenate([x_ref[r] * used, ones], axis=0)
        total = total + lax.dot_general(
            block, block, (((1,), (1,)), ((), ())), preferred_element_type=jnp.float32
        )
    out_ref[...] += total


def local_gram(smoothed, mask):
    rows, bands, cols = smoothed.shape
    per = 8
    return pl.pallas_call(
        gram_kernel,
        grid=(rows // per,),
        out_shape=jax.ShapeDtypeStruct((SIDE, SIDE), jnp.float32),
        in_specs=[
            pl.BlockSpec((per, bands, cols), lambda i: (i, 0, 0)),
            pl.BlockSpec((per, cols), lambda i: (i, 0)),
        ],
        out_specs=pl.BlockSpec((SIDE, SIDE), lambda i: (0, 0)),
        compiler_params=pltpu.CompilerParams(vmem_limit_bytes=40 << 20),
        name="local_gram",
    )(smoothed, mask)


def sum_kernel(
    na, nl, x_ref, out_ref, near, part, far, full, s1, r1, s2, r2, s3, r3, s4, r4
):
    ma, ml = lax.axis_index("across"), lax.axis_index("along")
    barrier = pltpu.get_barrier_semaphore()
    for axis, me, n in (("across", ma, na), ("along", ml, nl)):
        for d in range(1, n):
            pl.semaphore_signal(
                barrier, inc=1, device_id={axis: lax.rem(me + d, n)}, device_id_type=MESH_ID
            )
    pl.semaphore_wait(barrier, na - 1 + nl - 1)

    big = SIDE // na
    owners = min(nl, big // 8)
    small = big // owners

    def rows_of(start, count):
        return pl.ds(pl.multiple_of(start, 8), count)

    def copy(src, dst, send, recv, axis, peer):
        return pltpu.make_async_remote_copy(
            src_ref=src, dst_ref=dst, send_sem=send, recv_sem=recv,
            device_id={axis: peer}, device_id_type=MESH_ID,
        )

    def owner_only(index, action):
        if owners == nl:
            action()
        else:
            pl.when(index < owners)(action)

    one = []
    for d in range(1, na):
        peer = lax.rem(ma + d, na)
        one.append(copy(x_ref.at[rows_of(peer * big, big)], near.at[d - 1],
                        s1.at[d - 1], r1.at[d - 1], "across", peer))
    for c in one:
        c.start()
    for c in one:
        c.wait_recv()
    total = x_ref[rows_of(ma * big, big), :]
    for d in range(1, na):
        total = total + near[d - 1]
    part[...] = total

    two = []
    for d in range(1, nl):
        peer = lax.rem(ml + d, nl)
        slot = peer if owners == nl else lax.rem(peer, owners)
        two.append((peer, copy(part.at[rows_of(slot * small, small)], far.at[d - 1],
                               s2.at[d - 1], r2.at[d - 1], "along", peer)))
    for peer, c in two:
        owner_only(peer, c.start)

    mine = ml if owners == nl else lax.rem(ml, owners)
    here = rows_of(ma * big + mine * small, small)

    three = []
    for d in range(1, nl):
        peer = lax.rem(ml + d, nl)
        three.append(copy(full.at[here], full.at[here], s3.at[d - 1], r3.at[d - 1], "along", peer))

    def reduce_mine():
        for _, c in two:
            c.wait_recv()
        total = part[rows_of(mine * small, small), :]
        for d in range(1, nl):
            total = total + far[d - 1]
        full[here, :] = total
        for c in three:
            c.start()

    owner_only(ml, reduce_mine)
    for d in range(1, nl):
        owner_only(lax.rem(ml - d + nl, nl), three[d - 1].wait_recv)

    four = []
    block = rows_of(ma * big, big)
    for d in range(1, na):
        peer = lax.rem(ma + d, na)
        four.append(copy(full.at[block], full.at[block], s4.at[d - 1], r4.at[d - 1], "across", peer))
    for c in four:
        c.start()
    for c in four:
        c.wait_recv()
    out_ref[...] = full[...]
    for c in one:
        c.wait_send()
    for peer, c in two:
        owner_only(peer, c.wait_send)

    def sent():
        for c in three:
            c.wait_send()

    owner_only(ml, sent)
    for c in four:
        c.wait_send()


def sum_everywhere(gram):
    na, nl = lax.axis_size("across"), lax.axis_size("along")
    big = SIDE // na
    owners = min(nl, big // 8)
    dma = pltpu.SemaphoreType.DMA
    return pl.pallas_call(
        functools.partial(sum_kernel, na, nl),
        out_shape=jax.ShapeDtypeStruct(gram.shape, jnp.float32),
        in_specs=[pl.BlockSpec(memory_space=pltpu.VMEM)],
        out_specs=pl.BlockSpec(memory_space=pltpu.VMEM),
        scratch_shapes=[
            pltpu.VMEM((na - 1, big, SIDE), jnp.float32),
            pltpu.VMEM((big, SIDE), jnp.float32),
            pltpu.VMEM((nl - 1, big // owners, SIDE), jnp.float32),
            pltpu.VMEM((SIDE, SIDE), jnp.float32),
            dma((na - 1,)), dma((na - 1,)),
            dma((nl - 1,)), dma((nl - 1,)),
            dma((nl - 1,)), dma((nl - 1,)),
            dma((na - 1,)), dma((na - 1,)),
        ],
        compiler_params=pltpu.CompilerParams(collective_id=1, has_side_effects=True),
        name="sum_everywhere",
    )(gram)


def score_kernel(high_ref, low_ref, shift_ref, x_ref, mask_ref, out_ref):
    bands = high_ref.shape[0]
    for r in range(x_ref.shape[0]):
        x = x_ref[r]
        white = jnp.dot(high_ref[...], x, preferred_element_type=jnp.float32)
        white = white + jnp.dot(low_ref[...], x, preferred_element_type=jnp.float32)
        white = white - shift_ref[...]
        distance = jnp.sum(white * white, axis=0, keepdims=True)
        standard = (distance - bands) * (1.0 / math.sqrt(2.0 * bands))
        out_ref[r : r + 1, :] = standard * mask_ref[r : r + 1, :].astype(jnp.float32)


def score(whitener, mean, smoothed, mask):
    rows, bands, cols = smoothed.shape
    per = 8
    high = lax.reduce_precision(whitener, 8, 7)
    low = (whitener - high).astype(jnp.bfloat16)
    shift = jnp.dot(whitener, mean[:, None], precision=lax.Precision.HIGHEST)
    square = pl.BlockSpec((bands, bands), lambda i: (0, 0))
    lines = pl.BlockSpec((per, cols), lambda i: (i, 0))
    return pl.pallas_call(
        score_kernel,
        grid=(rows // per,),
        out_shape=jax.ShapeDtypeStruct((rows, cols), jnp.float32),
        in_specs=[
            square, square, pl.BlockSpec((bands, 1), lambda i: (0, 0)),
            pl.BlockSpec((per, bands, cols), lambda i: (i, 0, 0)), lines,
        ],
        out_specs=lines,
        compiler_params=pltpu.CompilerParams(vmem_limit_bytes=40 << 20),
        name="score",
    )(high.astype(jnp.bfloat16), low, shift, smoothed, mask)


def from_sides(low_edge, high_edge, axis):
    count = lax.axis_size(axis)
    forward = [(i, i + 1) for i in range(count - 1)]
    backward = [(i + 1, i) for i in range(count - 1)]
    return lax.ppermute(high_edge, axis, forward), lax.ppermute(low_edge, axis, backward)


def per_device(radiance, kernel_one, kernel_two, usable_mask):
    bands, rows, cols = radiance.shape
    na, nl = lax.axis_size("across"), lax.axis_size("along")
    ma, ml = lax.axis_index("across"), lax.axis_index("along")
    left, right = from_sides(radiance[:, :, :HALO], radiance[:, :, cols - HALO :], "across")
    above, below = from_sides(radiance[:, :HALO, :], radiance[:, rows - HALO :, :], "along")
    corner = jnp.concatenate([right, left], axis=2)
    corner_above, corner_below = from_sides(corner[:, :HALO], corner[:, rows - HALO :], "along")

    def widen(sides):
        gap = jnp.zeros(sides.shape[:2] + (128 - 2 * HALO,), sides.dtype)
        return jnp.concatenate([sides[:, :, :HALO], gap, sides[:, :, HALO:]], axis=2)

    edge = widen(corner)
    halo = jnp.concatenate(
        [jnp.concatenate([above, below], axis=1),
         widen(jnp.concatenate([corner_above, corner_below], axis=1))], axis=2)

    in_order, mid_order = row_orders(rows)
    first = tap_matrix(kernel_one, mid_order, in_order, ("high", "low"), 2 * len(in_order))
    packed = 3 * len(mid_order)
    second = tap_matrix(kernel_two, list(range(rows)), mid_order, ("high", "high", "low"),
                        packed + (-packed % 16))
    row_at = jnp.asarray([0 if r is None else r for r in mid_order], jnp.int32)[:, None]
    col_at = jnp.arange(cols + 128, dtype=jnp.int32)[None, :]
    col_at = jnp.where(col_at < cols + 64, col_at, col_at - cols - 128)
    row_at, col_at = row_at + ml * rows, col_at + ma * cols
    keep = (row_at >= 0) & (row_at < nl * rows) & (col_at >= 0) & (col_at < na * cols)
    smoothed = smooth_twice(radiance, halo, edge, first, second, keep.astype(jnp.float32))

    whole = sum_everywhere(local_gram(smoothed, usable_mask))
    gram, band_sum, count = whole[:bands, :bands], whole[bands, :bands], whole[bands, bands]
    mean = band_sum / count
    covariance = (gram - count * jnp.outer(mean, mean)) / (count - 1.0)
    loading = 0.01 * jnp.trace(covariance) / bands
    loaded = covariance + loading * jnp.eye(bands, dtype=jnp.float32)
    lower = jnp.linalg.cholesky(loaded)
    whitener = lax.linalg.triangular_solve(
        lower, jnp.eye(bands, dtype=jnp.float32), left_side=True, lower=True
    )
    return score(whitener, mean, smoothed, usable_mask)


def solution(mesh):
    in_specs = (P(None, "along", "across"), P(), P(), P("along", "across"))
    out_specs = P("along", "across")
    return jax.shard_map(
        per_device, mesh=mesh, in_specs=in_specs, out_specs=out_specs, check_vma=False
    )
```

```python
import functools
import math

import jax
import jax.numpy as jnp
import numpy as np
from jax import lax
from jax.experimental import pallas as pl
from jax.experimental.pallas import tpu as pltpu
from jax.sharding import PartitionSpec as P

KSIZE = 5
REACH = KSIZE // 2
HALO = 2 * REACH
GROUP = 16
SIDE = 256
MESH_ID = pl.DeviceIdType.MESH


def row_orders(rows):
    packed_in = list(range(rows)) + list(range(-HALO, 0)) + list(range(rows, rows + HALO))
    packed_mid = list(range(rows)) + list(range(-REACH, 0)) + list(range(rows, rows + REACH))
    packed_mid += [None] * (-len(packed_mid) % 8)
    return packed_in, packed_mid


LOW_AT, NONE_AT, LANES = 32, 127, 128


def tap_lanes(out_order, in_order, parts):
    lanes = np.full((KSIZE * len(out_order), LANES), NONE_AT, np.int32)
    for i, part in enumerate(parts):
        base = LOW_AT if part == "low" else 0
        for q in range(KSIZE):
            for m, r in enumerate(out_order):
                for k, s in enumerate(in_order):
                    if r is not None and s is not None and 0 <= s - r + REACH < KSIZE:
                        lanes[q * len(out_order) + m, i * len(in_order) + k] = (
                            base + (s - r + REACH) * KSIZE + q
                        )
    return jnp.asarray(lanes)


def tap_rows(kernel):
    high = lax.reduce_precision(kernel, 8, 7)
    low = kernel - high
    count = kernel.shape[1]
    row = jnp.pad(high, ((0, 0), (0, LOW_AT - count)))
    return jnp.concatenate([row, jnp.pad(low, ((0, 0), (0, LANES - LOW_AT - count)))], axis=1)


def tap_matrix(taps_ref, lanes_ref, b, width):
    row = jnp.broadcast_to(taps_ref[pl.ds(b, 1), :], lanes_ref.shape)
    matrix = jnp.take_along_axis(row, lanes_ref[...], axis=1, mode="promise_in_bounds")
    return matrix.astype(jnp.bfloat16)[:, :width]


def smooth_kernel(main_ref, halo_ref, edge_ref, one_ref, two_ref, first_ref, second_ref, keep_ref,
                  out_ref, hold):
    rows, cols = main_ref.shape[1:]
    wide = cols + edge_ref.shape[2]
    mid = keep_ref.shape[0]

    def gather_columns(product, count):
        total = product[REACH * count : (REACH + 1) * count, :]
        for q in range(KSIZE):
            if q != REACH:
                total = total + pltpu.roll(
                    product[q * count : (q + 1) * count, :], (REACH - q) % wide, 1
                )
        return total

    def one_band(b, carry):
        main = jnp.concatenate([main_ref[b], edge_ref[b]], axis=1).astype(jnp.float32)
        packed = jnp.concatenate([main, halo_ref[b].astype(jnp.float32)], axis=0)
        packed = jnp.concatenate([packed, packed], axis=0).astype(jnp.bfloat16)
        product = jnp.dot(tap_matrix(one_ref, first_ref, b, packed.shape[0]), packed,
                          preferred_element_type=jnp.float32)
        section = gather_columns(product, mid) * keep_ref[...]
        high = section.astype(jnp.bfloat16).astype(jnp.float32)
        low = section - high
        spare = -3 * mid % 16
        packed = jnp.concatenate(
            [high, low, high, jnp.zeros((spare, wide), jnp.float32)], axis=0
        ).astype(jnp.bfloat16)
        product = jnp.dot(tap_matrix(two_ref, second_ref, b, packed.shape[0]), packed,
                          preferred_element_type=jnp.float32)
        result = gather_columns(product, rows)
        for j in range(cols // 128):
            hold[j, pl.ds(pl.multiple_of(b * rows, rows), rows), :] = result[:, j * 128 : j * 128 + 128]
        return carry

    lax.fori_loop(0, GROUP, one_band, 0, unroll=4)
    for r in range(rows):
        for j in range(cols // 128):
            out_ref[r, :, j * 128 : j * 128 + 128] = hold[
                j, pl.ds(r, GROUP, stride=rows), :
            ].astype(jnp.bfloat16)


def smooth_twice(radiance, halo, edge, one, two, first, second, keep):
    bands, rows, cols = radiance.shape

    def band_block(array):
        return pl.BlockSpec((GROUP,) + array.shape[1:], lambda i: (i, 0, 0))

    return pl.pallas_call(
        smooth_kernel,
        grid=(bands // GROUP,),
        out_shape=jax.ShapeDtypeStruct((rows, bands, cols), jnp.bfloat16),
        in_specs=[band_block(a) for a in (radiance, halo, edge)]
        + [pl.BlockSpec((GROUP, LANES), lambda i: (i, 0))] * 2
        + [pl.BlockSpec(a.shape, lambda i: (0, 0)) for a in (first, second, keep)],
        out_specs=pl.BlockSpec((rows, GROUP, cols), lambda i: (0, i, 0)),
        scratch_shapes=[pltpu.VMEM((cols // 128, GROUP * rows, 128), jnp.float32)],
        compiler_params=pltpu.CompilerParams(vmem_limit_bytes=40 << 20),
        name="smooth_twice",
    )(radiance, halo, edge, one, two, first, second, keep)


def gram_kernel(x_ref, mask_ref, out_ref):
    step = pl.program_id(0)
    bands, cols = x_ref.shape[1:]
    per = x_ref.shape[0]

    @pl.when(step == 0)
    def _():
        out_ref[...] = jnp.zeros_like(out_ref)

    first = lax.broadcasted_iota(jnp.int32, (SIDE - bands, cols), 0) == 0
    total = jnp.zeros((SIDE, SIDE), jnp.float32)
    for r in range(per):
        line = mask_ref[r : r + 1, :].astype(jnp.float32)
        used = jnp.broadcast_to(line, (bands, cols)).astype(jnp.bfloat16)
        ones = jnp.where(first, jnp.broadcast_to(line, first.shape), 0.0).astype(jnp.bfloat16)
        block = jnp.concatenate([x_ref[r] * used, ones], axis=0)
        total = total + lax.dot_general(
            block, block, (((1,), (1,)), ((), ())), preferred_element_type=jnp.float32
        )
    out_ref[...] += total


def local_gram(smoothed, mask):
    rows, bands, cols = smoothed.shape
    per = 8
    return pl.pallas_call(
        gram_kernel,
        grid=(rows // per,),
        out_shape=jax.ShapeDtypeStruct((SIDE, SIDE), jnp.float32),
        in_specs=[
            pl.BlockSpec((per, bands, cols), lambda i: (i, 0, 0)),
            pl.BlockSpec((per, cols), lambda i: (i, 0)),
        ],
        out_specs=pl.BlockSpec((SIDE, SIDE), lambda i: (0, 0)),
        compiler_params=pltpu.CompilerParams(vmem_limit_bytes=40 << 20),
        name="local_gram",
    )(smoothed, mask)


def sum_kernel(
    na, nl, x_ref, out_ref, near, part, far, full, s1, r1, s2, r2, s3, r3, s4, r4
):
    ma, ml = lax.axis_index("across"), lax.axis_index("along")
    barrier = pltpu.get_barrier_semaphore()
    for axis, me, n in (("across", ma, na), ("along", ml, nl)):
        for d in range(1, n):
            pl.semaphore_signal(
                barrier, inc=1, device_id={axis: lax.rem(me + d, n)}, device_id_type=MESH_ID
            )
    pl.semaphore_wait(barrier, na - 1 + nl - 1)

    big = SIDE // na
    owners = min(nl, big // 8)
    small = big // owners

    def rows_of(start, count):
        return pl.ds(pl.multiple_of(start, 8), count)

    def copy(src, dst, send, recv, axis, peer):
        return pltpu.make_async_remote_copy(
            src_ref=src, dst_ref=dst, send_sem=send, recv_sem=recv,
            device_id={axis: peer}, device_id_type=MESH_ID,
        )

    def owner_only(index, action):
        if owners == nl:
            action()
        else:
            pl.when(index < owners)(action)

    one = []
    for d in range(1, na):
        peer = lax.rem(ma + d, na)
        one.append(copy(x_ref.at[rows_of(peer * big, big)], near.at[d - 1],
                        s1.at[d - 1], r1.at[d - 1], "across", peer))
    for c in one:
        c.start()
    for c in one:
        c.wait_recv()
    total = x_ref[rows_of(ma * big, big), :]
    for d in range(1, na):
        total = total + near[d - 1]
    part[...] = total

    two = []
    for d in range(1, nl):
        peer = lax.rem(ml + d, nl)
        slot = peer if owners == nl else lax.rem(peer, owners)
        two.append((peer, copy(part.at[rows_of(slot * small, small)], far.at[d - 1],
                               s2.at[d - 1], r2.at[d - 1], "along", peer)))
    for peer, c in two:
        owner_only(peer, c.start)

    mine = ml if owners == nl else lax.rem(ml, owners)
    here = rows_of(ma * big + mine * small, small)

    three = []
    for d in range(1, nl):
        peer = lax.rem(ml + d, nl)
        three.append(copy(full.at[here], full.at[here], s3.at[d - 1], r3.at[d - 1], "along", peer))

    def reduce_mine():
        for _, c in two:
            c.wait_recv()
        total = part[rows_of(mine * small, small), :]
        for d in range(1, nl):
            total = total + far[d - 1]
        full[here, :] = total
        for c in three:
            c.start()

    owner_only(ml, reduce_mine)
    for d in range(1, nl):
        owner_only(lax.rem(ml - d + nl, nl), three[d - 1].wait_recv)

    four = []
    block = rows_of(ma * big, big)
    for d in range(1, na):
        peer = lax.rem(ma + d, na)
        four.append(copy(full.at[block], full.at[block], s4.at[d - 1], r4.at[d - 1], "across", peer))
    for c in four:
        c.start()
    for c in four:
        c.wait_recv()
    out_ref[...] = full[...]
    for c in one:
        c.wait_send()
    for peer, c in two:
        owner_only(peer, c.wait_send)

    def sent():
        for c in three:
            c.wait_send()

    owner_only(ml, sent)
    for c in four:
        c.wait_send()


def sum_everywhere(gram):
    na, nl = lax.axis_size("across"), lax.axis_size("along")
    big = SIDE // na
    owners = min(nl, big // 8)
    dma = pltpu.SemaphoreType.DMA
    return pl.pallas_call(
        functools.partial(sum_kernel, na, nl),
        out_shape=jax.ShapeDtypeStruct(gram.shape, jnp.float32),
        in_specs=[pl.BlockSpec(memory_space=pltpu.VMEM)],
        out_specs=pl.BlockSpec(memory_space=pltpu.VMEM),
        scratch_shapes=[
            pltpu.VMEM((na - 1, big, SIDE), jnp.float32),
            pltpu.VMEM((big, SIDE), jnp.float32),
            pltpu.VMEM((nl - 1, big // owners, SIDE), jnp.float32),
            pltpu.VMEM((SIDE, SIDE), jnp.float32),
            dma((na - 1,)), dma((na - 1,)),
            dma((nl - 1,)), dma((nl - 1,)),
            dma((nl - 1,)), dma((nl - 1,)),
            dma((na - 1,)), dma((na - 1,)),
        ],
        compiler_params=pltpu.CompilerParams(collective_id=1, has_side_effects=True),
        name="sum_everywhere",
    )(gram)


def score_kernel(high_ref, low_ref, shift_ref, x_ref, mask_ref, out_ref):
    bands = high_ref.shape[0]
    for r in range(x_ref.shape[0]):
        x = x_ref[r]
        white = jnp.dot(high_ref[...], x, preferred_element_type=jnp.float32)
        white = white + jnp.dot(low_ref[...], x, preferred_element_type=jnp.float32)
        white = white - shift_ref[...]
        distance = jnp.sum(white * white, axis=0, keepdims=True)
        standard = (distance - bands) * (1.0 / math.sqrt(2.0 * bands))
        out_ref[r : r + 1, :] = standard * mask_ref[r : r + 1, :].astype(jnp.float32)


def score(whitener, mean, smoothed, mask):
    rows, bands, cols = smoothed.shape
    per = 8
    high = lax.reduce_precision(whitener, 8, 7)
    low = (whitener - high).astype(jnp.bfloat16)
    shift = jnp.dot(whitener, mean[:, None], precision=lax.Precision.HIGHEST)
    square = pl.BlockSpec((bands, bands), lambda i: (0, 0))
    lines = pl.BlockSpec((per, cols), lambda i: (i, 0))
    return pl.pallas_call(
        score_kernel,
        grid=(rows // per,),
        out_shape=jax.ShapeDtypeStruct((rows, cols), jnp.float32),
        in_specs=[
            square, square, pl.BlockSpec((bands, 1), lambda i: (0, 0)),
            pl.BlockSpec((per, bands, cols), lambda i: (i, 0, 0)), lines,
        ],
        out_specs=lines,
        compiler_params=pltpu.CompilerParams(vmem_limit_bytes=40 << 20),
        name="score",
    )(high.astype(jnp.bfloat16), low, shift, smoothed, mask)


def from_sides(low_edge, high_edge, axis):
    count = lax.axis_size(axis)
    forward = [(i, i + 1) for i in range(count - 1)]
    backward = [(i + 1, i) for i in range(count - 1)]
    return lax.ppermute(high_edge, axis, forward), lax.ppermute(low_edge, axis, backward)


def per_device(radiance, kernel_one, kernel_two, usable_mask):
    bands, rows, cols = radiance.shape
    na, nl = lax.axis_size("across"), lax.axis_size("along")
    ma, ml = lax.axis_index("across"), lax.axis_index("along")
    left, right = from_sides(radiance[:, :, :HALO], radiance[:, :, cols - HALO :], "across")
    above, below = from_sides(radiance[:, :HALO, :], radiance[:, rows - HALO :, :], "along")
    corner = jnp.concatenate([right, left], axis=2)
    corner_above, corner_below = from_sides(corner[:, :HALO], corner[:, rows - HALO :], "along")

    def widen(sides):
        gap = jnp.zeros(sides.shape[:2] + (128 - 2 * HALO,), sides.dtype)
        return jnp.concatenate([sides[:, :, :HALO], gap, sides[:, :, HALO:]], axis=2)

    edge = widen(corner)
    halo = jnp.concatenate(
        [jnp.concatenate([above, below], axis=1),
         widen(jnp.concatenate([corner_above, corner_below], axis=1))], axis=2)

    in_order, mid_order = row_orders(rows)
    first = tap_lanes(mid_order, in_order, ("high", "low"))
    second = tap_lanes(list(range(rows)), mid_order, ("high", "high", "low"))
    row_at = jnp.asarray([0 if r is None else r for r in mid_order], jnp.int32)[:, None]
    col_at = jnp.arange(cols + 128, dtype=jnp.int32)[None, :]
    col_at = jnp.where(col_at < cols + 64, col_at, col_at - cols - 128)
    row_at, col_at = row_at + ml * rows, col_at + ma * cols
    keep = (row_at >= 0) & (row_at < nl * rows) & (col_at >= 0) & (col_at < na * cols)
    smoothed = smooth_twice(
        radiance, halo, edge, tap_rows(kernel_one), tap_rows(kernel_two), first, second,
        keep.astype(jnp.float32),
    )

    whole = sum_everywhere(local_gram(smoothed, usable_mask))
    gram, band_sum, count = whole[:bands, :bands], whole[bands, :bands], whole[bands, bands]
    mean = band_sum / count
    covariance = (gram - count * jnp.outer(mean, mean)) / (count - 1.0)
    loading = 0.01 * jnp.trace(covariance) / bands
    loaded = covariance + loading * jnp.eye(bands, dtype=jnp.float32)
    lower = jnp.linalg.cholesky(loaded)
    whitener = lax.linalg.triangular_solve(
        lower, jnp.eye(bands, dtype=jnp.float32), left_side=True, lower=True
    )
    return score(whitener, mean, smoothed, usable_mask)


def solution(mesh):
    in_specs = (P(None, "along", "across"), P(), P(), P("along", "across"))
    out_specs = P("along", "across")
    return jax.shard_map(
        per_device, mesh=mesh, in_specs=in_specs, out_specs=out_specs, check_vma=False
    )
```
